32 devices in a mesh: ctx: 4 (over x, core), row: 4 (over z), col: 2 (over y).
Axes of the slice: x: 2, y: 2, z: 4, core: 2. Of those that a mesh axis runs over, the one named last changes fastest.
Arguments:
- inputs: bfloat16 [1024, 4096], P('ctx', 'col'), may hold values from -12 to 12
- qkv_weight: bfloat16 [4096, 6144], P('col', 'row'), may hold values from -0.140625 to 0.140625
- out_cotangent: bfloat16 [1024, 2048], P('ctx', ('row', 'col')), may hold values from -6 to 6
Outputs:
- attended: bfloat16 [1024, 2048], P('ctx', ('row', 'col'))
- input_grad: bfloat16 [1024, 4096], P('ctx', 'col')
The draws below stay inside these ranges and needn't reach their ends.
All inputs are finite; a program needn't handle non-finite values.
Results may differ from the reference program's by a relative error of at most 0.0173.
The reference program's roundings to bfloat16 on the way count: a program that leaves them out, or rounds other values in their place, can miss the bound.
Values may be sent and summed in bfloat16 or wider, within the bound.
A program may use at most 128 MiB of HBM per device.

```python
import math
import jax
import jax.numpy as jnp
from jax import lax

D = 4096
HEADS = 16
DH = 128
TOKENS = 1024


def draw_inputs(key, part):
    key = jax.random.fold_in(key, 11)
    base_key = jax.random.fold_in(key, 0)
    values = jnp.clip(jax.random.normal(base_key, (TOKENS, D), jnp.float32), -6.0, 6.0)
    return values.astype(jnp.bfloat16)


def draw_qkv_weight(key, part):
    key = jax.random.fold_in(key, 23)
    own_key = jax.random.fold_in(key, 1)
    own = jnp.clip(jax.random.normal(own_key, (D, HEADS, 3, DH), jnp.float32), -6.0, 6.0)
    return (own / math.sqrt(D)).reshape(D, 3 * HEADS * DH).astype(jnp.bfloat16)


def shard_levels(rng, dims, cuts, smallest, largest):
    factor_of, own = 1.0, jax.random.fold_in(rng, 6)
    for position, shards_of in cuts:
        heights = jnp.exp(jax.random.uniform(jax.random.fold_in(own, position), (shards_of,), jnp.float32, smallest / len(cuts), largest / len(cuts)))
        factor_of = factor_of * jnp.repeat(heights, dims[position] // shards_of).reshape([-1 if axis == position else 1 for axis in range(len(dims))])
    return factor_of


def centred(stream_key, shape, deviation, reach, pieces=(), kind=jnp.bfloat16):
    factor_of = shard_levels(stream_key, shape, pieces, -0.22, 0.18) if pieces else 1.0
    values = jax.random.normal(stream_key, shape, jnp.float32) * deviation * factor_of
    return jnp.minimum(jnp.maximum(values, -reach), reach).astype(kind)


def setup_inputs(seed: int = 0) -> dict:
    seeds = jax.random.split(jax.random.key(seed), 4)
    inputs = draw_inputs(jax.random.fold_in(seeds[3], 71), 0)
    qkv_weight = draw_qkv_weight(jax.random.fold_in(seeds[3], 71), 0)
    out_cotangent = centred(seeds[2], (TOKENS, HEADS * DH), 1.0, 6.0, ((0, 4), (1, 8)))
    return dict(inputs=inputs, qkv_weight=qkv_weight, out_cotangent=out_cotangent)


def attend_head(queries, keys_head, values_head, grad_out):
    scaling = 1.0 / math.sqrt(DH)
    scores = jnp.dot(queries, keys_head.T, preferred_element_type=jnp.float32) * scaling
    row_max = lax.optimization_barrier(jnp.max(scores, axis=1, keepdims=True))
    expo_vals = jnp.exp(scores - row_max)
    row_total = lax.optimization_barrier(jnp.sum(expo_vals, axis=1, keepdims=True))
    softmax = expo_vals / row_total
    softmax_low = softmax.astype(jnp.bfloat16)
    attended = jnp.dot(softmax_low, values_head, preferred_element_type=jnp.float32).astype(jnp.bfloat16)
    row_delta = lax.optimization_barrier(jnp.sum(grad_out.astype(jnp.float32) * attended.astype(jnp.float32), axis=1, keepdims=True))
    grad_soft = jnp.dot(grad_out, values_head.T, preferred_element_type=jnp.float32)
    grad_score = (softmax * (grad_soft - row_delta)).astype(jnp.bfloat16)
    grad_query = (jnp.dot(grad_score, keys_head, preferred_element_type=jnp.float32) * scaling).astype(jnp.bfloat16)
    grad_key = (jnp.dot(grad_score.T, queries, preferred_element_type=jnp.float32) * scaling).astype(jnp.bfloat16)
    grad_value = jnp.dot(softmax_low.T, grad_out, preferred_element_type=jnp.float32).astype(jnp.bfloat16)
    return (attended, grad_query, grad_key, grad_value)

def reference(inputs, qkv_weight, out_cotangent):
    qkv = jnp.dot(inputs, qkv_weight, preferred_element_type=jnp.float32).astype(jnp.bfloat16)
    per_head = jnp.transpose(qkv.reshape(TOKENS, HEADS, 3, DH), (1, 2, 0, 3))
    grad_heads = jnp.transpose(out_cotangent.reshape(TOKENS, HEADS, DH), (1, 0, 2))

    def one_head(operands):
        block, grad_out = operands
        return attend_head(block[0], block[1], block[2], grad_out)
    attended, grad_query, grad_key, grad_value = lax.map(one_head, (per_head, grad_heads))
    attended = jnp.transpose(attended, (1, 0, 2)).reshape(TOKENS, HEADS * DH)
    grad_qkv = jnp.stack([grad_query, grad_key, grad_value], axis=2)
    grad_qkv = jnp.transpose(grad_qkv, (1, 0, 2, 3)).reshape(TOKENS, 3 * HEADS * DH)
    input_grad = jnp.dot(grad_qkv, qkv_weight.T, preferred_element_type=jnp.float32).astype(jnp.bfloat16)
    return (attended, input_grad)
```

```python
import math

import jax
import jax.numpy as jnp
from jax import lax
from jax.experimental import pallas as pl
from jax.experimental.pallas import tpu as pltpu
from jax.sharding import PartitionSpec as P

DH = 128


def softmax_rows(scores):
    row_top = jnp.max(scores, axis=2)
    expo_vals = jnp.exp(scores - row_top[:, :, None])
    row_total = jnp.sum(expo_vals, axis=2)
    return (row_top, row_total, expo_vals / row_total[:, :, None])


def shards(inputs, qkv_weight, out_cotangent):
    tok_rows = inputs.shape[0]
    scaling = 1.0 / math.sqrt(DH)
    per_device = qkv_weight.shape[1] // lax.axis_size("col")
    local_heads = per_device // (3 * DH)
    panel_cols = qkv_weight
    packed = lax.psum_scatter(
        lax.dot_general(
            panel_cols, inputs, (((0,), (1,)), ((), ())), preferred_element_type=jnp.float32
        ),
        "col",
        scatter_dimension=0,
        tiled=True,
    ).astype(jnp.bfloat16)
    packed = packed.reshape(local_heads, 3, DH, tok_rows)
    queries = packed[:, 0]
    key_own = packed[:, 1]
    value_own = packed[:, 2]
    gathered = lax.all_gather(jnp.stack([key_own, value_own]), "ctx", axis=3, tiled=True)
    keys_all = gathered[0]
    values_all = gathered[1]
    scores = (
        jnp.einsum("hdq,hdk->hqk", queries, keys_all, preferred_element_type=jnp.float32) * scaling
    )
    row_top, row_total, softmax = softmax_rows(scores)
    softmax_low = softmax.astype(jnp.bfloat16)
    attended3 = jnp.einsum(
        "hqk,hdk->qhd", softmax_low, values_all, preferred_element_type=jnp.float32
    ).astype(jnp.bfloat16)
    attended = attended3.reshape(tok_rows, local_heads * DH)
    grad_out = out_cotangent.reshape(tok_rows, local_heads, DH)
    row_delta = jnp.sum(grad_out.astype(jnp.float32) * attended3.astype(jnp.float32), axis=2).T
    grad_soft = jnp.einsum("qhd,hdk->hqk", grad_out, values_all, preferred_element_type=jnp.float32)
    grad_score = (softmax * (grad_soft - row_delta[:, :, None])).astype(jnp.bfloat16)
    grad_query = (
        jnp.einsum("hqk,hdk->hdq", grad_score, keys_all, preferred_element_type=jnp.float32)
        * scaling
    ).astype(jnp.bfloat16)
    grad_out_t = jnp.transpose(grad_out, (1, 2, 0))
    stat_top, stat_total, stat_delta = (
        lax.all_gather(row_top, "ctx", axis=1, tiled=True),
        lax.all_gather(row_total, "ctx", axis=1, tiled=True),
        lax.all_gather(row_delta, "ctx", axis=1, tiled=True),
    )
    query_part = lax.all_gather(queries, "ctx", axis=2, tiled=True)
    grad_part = lax.all_gather(grad_out_t, "ctx", axis=2, tiled=True)
    part_scores = (
        jnp.einsum("hdq,hdk->hqk", query_part, key_own, preferred_element_type=jnp.float32)
        * scaling
    )
    part_prob = jnp.exp(part_scores - stat_top[:, :, None]) / stat_total[:, :, None]
    part_grad = jnp.einsum("hdq,hdk->hqk", grad_part, value_own, preferred_element_type=jnp.float32)
    part_score = (part_prob * (part_grad - stat_delta[:, :, None])).astype(jnp.bfloat16)
    new_key = (
        jnp.einsum("hqk,hdq->hdk", part_score, query_part, preferred_element_type=jnp.float32)
        * scaling
    )
    new_value = jnp.einsum(
        "hqk,hdq->hdk",
        part_prob.astype(jnp.bfloat16),
        grad_part,
        preferred_element_type=jnp.float32,
    )
    grad_key = new_key
    grad_value = new_value
    grad_key = grad_key.astype(jnp.bfloat16)
    grad_value = grad_value.astype(jnp.bfloat16)
    grad_packed = jnp.stack([grad_query, grad_key, grad_value], axis=1).reshape(
        local_heads * 3 * DH, tok_rows
    )
    panel_cols = qkv_weight
    local_sum = lax.dot_general(
        lax.all_gather(grad_packed, "col", axis=0, tiled=True),
        panel_cols,
        (((0,), (1,)), ((), ())),
        preferred_element_type=jnp.float32,
    )
    input_grad = lax.psum(local_sum, "row").astype(jnp.bfloat16)
    return (attended, input_grad)


MESH = pl.DeviceIdType.MESH
CHUNKS = 16
NN = (((1,), (0,)), ((), ()))
NT = (((1,), (1,)), ((), ()))
TN = (((0,), (0,)), ((), ()))


def dot(a, b, dims):
    return lax.dot_general(a, b, dims, preferred_element_type=jnp.float32)


def block_kernel(
    x_hbm, w_hbm, cot_hbm, att_ref, grad_ref,
    x_ref, w_ref, cot_ref, far_kv, far_q, got_kv, got_q, part_near, got_near, cot_all, query, kv, score, gscore,
    prob_low, ds_low, att_mine, att_send, att_got, dq_send, dkv_send, dkv_got, dkv_own,
    dkv_out, packed, z_own, z_edge, z_mid, z_tot, ss, rs, zs, zr, ls,
):
    tok = x_hbm.shape[0]
    head = 3 * DH
    scaling = 1.0 / math.sqrt(DH)
    ctx, row, col = lax.axis_index("ctx"), lax.axis_index("row"), lax.axis_index("col")
    core = lax.rem(ctx, 2)
    far_x = lax.rem(ctx + 2, 4)
    near = ctx + 1 - 2 * core
    far_col = 1 - col
    is_mid = jnp.logical_or(row == 1, row == 2)
    mid_peer = 3 - row
    side = jnp.where(row == 0, 1, jnp.where(row == 1, 0, jnp.where(row == 2, 3, 2)))
    at_near = {"ctx": near, "row": row, "col": col}
    at_far = {"ctx": ctx, "row": row, "col": far_col}
    at_diag = {"ctx": near, "row": row, "col": far_col}
    at_x = {"ctx": far_x, "row": row, "col": col}
    at_side = {"ctx": ctx, "row": side, "col": col}
    at_mid = {"ctx": ctx, "row": mid_peer, "col": col}

    def rc(src, dst, n, dev):
        return pltpu.make_async_remote_copy(
            src_ref=src, dst_ref=dst, send_sem=ss.at[n], recv_sem=rs.at[n],
            device_id=dev, device_id_type=MESH,
        )

    def lanes(start, size):
        return pl.ds(pl.multiple_of(start, 128), size)

    far_w = lanes(far_col * 2 * head, 2 * head)
    own_w = lanes(col * 2 * head, 2 * head)
    loads = [
        pltpu.make_async_copy(x_hbm, x_ref, ls.at[0]),
        pltpu.make_async_copy(w_hbm.at[:, far_w], w_ref.at[:, far_w], ls.at[1]),
        pltpu.make_async_copy(w_hbm.at[:, own_w], w_ref.at[:, own_w], ls.at[2]),
        pltpu.make_async_copy(cot_hbm, cot_ref, ls.at[3]),
    ]
    for load in loads:
        load.start()
    barrier = pltpu.get_barrier_semaphore()
    for dev in (at_near, at_far, at_diag, at_x, at_side):
        pl.semaphore_signal(barrier, inc=1, device_id=dev, device_id_type=MESH)

    @pl.when(is_mid)
    def _():
        pl.semaphore_signal(barrier, inc=1, device_id=at_mid, device_id_type=MESH)

    loads[0].wait()
    loads[1].wait()
    far = dot(x_ref[...], w_ref[:, far_w], NN)
    for n in range(2):
        far_q[n] = far[:, n * head : n * head + DH]
        far_kv[n] = far[:, n * head + DH : (n + 1) * head]

    @pl.when(is_mid)
    def _():
        pl.semaphore_wait(barrier, 6)

    @pl.when(jnp.logical_not(is_mid))
    def _():
        pl.semaphore_wait(barrier, 5)

    sent = []

    def go(copy):
        copy.start()
        sent.append(copy)
        return copy

    kv_copies = [go(rc(far_kv.at[core], got_kv.at[0], 0, at_far))]
    kv_copies.append(go(rc(far_kv.at[1 - core], got_kv.at[1], 1, at_diag)))
    q_copies = [go(rc(far_q.at[core], got_q.at[0], 15, at_far))]
    q_copies.append(go(rc(far_q.at[1 - core], got_q.at[1], 16, at_diag)))
    loads[3].wait()
    cc = go(rc(cot_ref.at[:, lanes((1 - core) * DH, DH)], cot_all.at[pl.ds(tok, tok)], 3, at_near))
    loads[2].wait()
    own = dot(x_ref[...], w_ref[:, own_w], NN)
    part_near[0] = own[:, :head]
    part_near[1] = own[:, head:]
    near_copy = go(rc(part_near.at[1 - core], got_near, 2, at_near))
    cot_all[pl.ds(0, tok), :] = cot_ref[:, lanes(core * DH, DH)]

    kv_sent = []
    for t in range(2):
        kv_copies[t].wait_recv()
        if t == 0:
            mine = part_near[core, :, DH:]
        else:
            near_copy.wait_recv()
            mine = got_near[:, DH:]
        here = pl.ds(t * tok, tok)
        kv[here, :] = (mine + got_kv[t]).astype(jnp.bfloat16)
        kv_sent.append(go(rc(kv.at[here], kv.at[pl.ds((2 + t) * tok, tok)], 4 + t, at_x)))

    cc.wait_recv()
    near_keys = pl.ds(0, 2 * tok)
    far_keys = pl.ds(2 * tok, 2 * tok)
    gscore[:, near_keys] = dot(cot_all[...], kv[near_keys, DH:], NT)
    for t in range(2):
        q_copies[t].wait_recv()
        mine = part_near[core, :, :DH] if t == 0 else got_near[:, :DH]
        query[pl.ds(t * tok, tok), :] = (mine + got_q[t]).astype(jnp.bfloat16)
    score[:, near_keys] = dot(query[...], kv[near_keys, :DH], NT) * scaling
    for t in range(2):
        kv_sent[t].wait_recv()
    gscore[:, far_keys] = dot(cot_all[...], kv[far_keys, DH:], NT)
    score[:, far_keys] = dot(query[...], kv[far_keys, :DH], NT) * scaling

    mine_lane = (2 * col + core) * head
    part = tok // 2
    for t in (1, 0):
        for half in range(2):
            here = pl.ds(t * tok + half * part, part)
            local = pl.ds(half * part, part)
            s = score[here, :]
            e = jnp.exp(s - jnp.max(s, axis=1, keepdims=True))
            p = e * (1.0 / jnp.sum(e, axis=1, keepdims=True))
            low = p.astype(jnp.bfloat16)
            prob_low[here, :] = low
            att = dot(low, kv[:, DH:], NN).astype(jnp.bfloat16)
            delta = jnp.sum(
                cot_all[here, :].astype(jnp.float32) * att.astype(jnp.float32), axis=1, keepdims=True
            )
            ds = (p * (gscore[here, :] - delta)).astype(jnp.bfloat16)
            ds_low[here, :] = ds
            dq_send[here, :] = (dot(ds, kv[:, :DH], NN) * scaling).astype(jnp.bfloat16)
            if t == 1:
                att_send[local, :] = att
            else:
                att_mine[local, :] = att
        here = pl.ds(t * tok, tok)
        slot = packed.at[:, lanes(mine_lane, DH)]
        if t == 1:
            go(rc(dq_send.at[here], slot, 9, at_diag))
            go(rc(dq_send.at[here], slot, 10, at_near))
            att_copy = go(rc(att_send, att_got, 8, at_near))
        else:
            go(rc(dq_send.at[here], slot, 11, at_far))
            packed[:, lanes(mine_lane, DH)] = dq_send[here, :]

    dkv_copies = []
    for t in range(2):
        keys = pl.ds((2 + t) * tok, tok)
        here = pl.ds(t * tok, tok)
        dkv_send[here, :DH] = (dot(ds_low[:, keys], query[...], TN) * scaling).astype(jnp.bfloat16)
        dkv_send[here, DH:] = dot(prob_low[:, keys], cot_all[...], TN).astype(jnp.bfloat16)
        dkv_copies.append(go(rc(dkv_send.at[here], dkv_got.at[here], 6 + t, at_x)))
    dkv_own[:, :DH] = dot(ds_low[:, near_keys], query[...], TN) * scaling
    dkv_own[:, DH:] = dot(prob_low[:, near_keys], cot_all[...], TN)
    att_copy.wait_recv()
    att_ref[:, lanes(core * DH, DH)] = att_mine[...]
    att_ref[:, lanes((1 - core) * DH, DH)] = att_got[...]
    slot = packed.at[:, lanes(mine_lane + DH, 2 * DH)]
    for t in (0, 1):
        here = pl.ds(t * tok, tok)
        dkv_copies[t].wait_recv()
        dkv_out[here, :] = (dkv_own[here, :] + dkv_got[here, :].astype(jnp.float32)).astype(jnp.bfloat16)
        if t == 1:
            go(rc(dkv_out.at[here], slot, 12, at_diag))
            go(rc(dkv_out.at[here], slot, 13, at_near))
        else:
            go(rc(dkv_out.at[here], slot, 14, at_far))
            packed[:, lanes(mine_lane + DH, 2 * DH)] = dkv_out[here, :]

    near_lane = (2 * col + 1 - core) * head
    far_lane = (2 * far_col + core) * head
    diag_lane = (2 * far_col + 1 - core) * head
    for n_q, n_kv, lane, dev in (
        (10, 13, near_lane, at_near), (11, 14, far_lane, at_far), (9, 12, diag_lane, at_diag)
    ):
        to = packed.at[:, lanes(lane, DH)]
        rc(to, to, n_q, dev).wait_recv()
        to = packed.at[:, lanes(lane + DH, 2 * DH)]
        rc(to, to, n_kv, dev).wait_recv()

    width = grad_ref.shape[1] // CHUNKS

    def zcopy(kind, src, dst, k, dev):
        return pltpu.make_async_remote_copy(
            src_ref=src.at[k], dst_ref=dst.at[k], send_sem=zs.at[kind, k], recv_sem=zr.at[kind, k],
            device_id=dev, device_id_type=MESH,
        )

    def product(k):
        rows = pl.ds(pl.multiple_of(k * width, width), width)
        return dot(packed[...], w_ref[rows, :], NT)

    def put(k, value):
        grad_ref[:, lanes(k * width, width)] = value

    @pl.when(jnp.logical_not(is_mid))
    def _():
        @pl.loop(0, CHUNKS)
        def _(k):
            z_own[k] = product(k).astype(jnp.bfloat16)
            zcopy(0, z_own, z_edge, k, at_side).start()

        @pl.loop(0, CHUNKS)
        def _(k):
            zcopy(2, z_tot, z_tot, k, at_side).wait_recv()
            put(k, z_tot[k])
            zcopy(0, z_own, z_edge, k, at_side).wait_send()

    @pl.when(is_mid)
    def _():
        def finish(k):
            zcopy(1, z_own, z_mid, k, at_mid).wait_recv()
            total = (z_own[k].astype(jnp.float32) + z_mid[k].astype(jnp.float32)).astype(jnp.bfloat16)
            z_tot[k] = total
            zcopy(2, z_tot, z_tot, k, at_side).start()
            put(k, total)

        @pl.loop(0, CHUNKS)
        def _(k):
            term = product(k)
            zcopy(0, z_own, z_edge, k, at_side).wait_recv()
            z_own[k] = (term + z_edge[k].astype(jnp.float32)).astype(jnp.bfloat16)
            zcopy(1, z_own, z_mid, k, at_mid).start()

            @pl.when(k > 0)
            def _():
                finish(k - 1)

        finish(CHUNKS - 1)

        @pl.loop(0, CHUNKS)
        def _(k):
            zcopy(1, z_own, z_mid, k, at_mid).wait_send()
            zcopy(2, z_tot, z_tot, k, at_side).wait_send()

    for copy in sent:
        copy.wait_send()


def fused(inputs, qkv_weight, out_cotangent):
    tok, wide = inputs.shape
    low, full = jnp.bfloat16, jnp.float32
    head = 3 * DH
    chunk = (CHUNKS, tok, wide // CHUNKS)
    vmem = pl.BlockSpec(memory_space=pltpu.VMEM)
    shapes = [
        (inputs.shape, low), (qkv_weight.shape, low), (out_cotangent.shape, low),
        ((2, tok, 2 * DH), full), ((2, tok, DH), full), ((2, tok, 2 * DH), full), ((2, tok, DH), full),
        ((2, tok, head), full), ((tok, head), full),
        ((2 * tok, DH), low), ((2 * tok, DH), low), ((4 * tok, 2 * DH), low),
        ((2 * tok, 4 * tok), full), ((2 * tok, 4 * tok), full),
        ((2 * tok, 4 * tok), low), ((2 * tok, 4 * tok), low),
        ((tok, DH), low), ((tok, DH), low), ((tok, DH), low), ((2 * tok, DH), low),
        ((2 * tok, 2 * DH), low), ((2 * tok, 2 * DH), low), ((2 * tok, 2 * DH), full),
        ((2 * tok, 2 * DH), low), ((tok, 4 * head), low),
        (chunk, low), (chunk, low), (chunk, low), (chunk, low),
    ]
    return pl.pallas_call(
        block_kernel,
        out_shape=(
            jax.ShapeDtypeStruct(out_cotangent.shape, low),
            jax.ShapeDtypeStruct(inputs.shape, low),
        ),
        in_specs=[pl.BlockSpec(memory_space=pl.ANY)] * 3,
        out_specs=(vmem, vmem),
        scratch_shapes=[pltpu.VMEM(shape, kind) for shape, kind in shapes]
        + [pltpu.SemaphoreType.DMA((17,))] * 2
        + [pltpu.SemaphoreType.DMA((3, CHUNKS))] * 2
        + [pltpu.SemaphoreType.DMA((4,))],
        compiler_params=pltpu.CompilerParams(
            collective_id=0, has_side_effects=True, vmem_limit_bytes=62 * 1024 * 1024
        ),
    )(inputs, qkv_weight, out_cotangent)


def block(inputs, qkv_weight, out_cotangent):
    sizes = tuple(lax.axis_size(name) for name in ("ctx", "row", "col"))
    heads = qkv_weight.shape[1] // (3 * DH)
    if sizes == (4, 4, 2) and heads == 4 and inputs.shape[0] <= 256:
        return fused(inputs, qkv_weight, out_cotangent)
    return shards(inputs, qkv_weight, out_cotangent)


def solution(mesh):
    return jax.shard_map(
        block,
        mesh=mesh,
        in_specs=(P("ctx", "col"), P("col", "row"), P("ctx", ("row", "col"))),
        out_specs=(P("ctx", ("row", "col")), P("ctx", "col")),
        check_vma=False,
    )
```

```python
import math

import jax
import jax.numpy as jnp
from jax import lax
from jax.experimental import pallas as pl
from jax.experimental.pallas import tpu as pltpu
from jax.sharding import PartitionSpec as P

DH = 128


def softmax_rows(scores):
    row_top = jnp.max(scores, axis=2)
    expo_vals = jnp.exp(scores - row_top[:, :, None])
    row_total = jnp.sum(expo_vals, axis=2)
    return (row_top, row_total, expo_vals / row_total[:, :, None])


def shards(inputs, qkv_weight, out_cotangent):
    tok_rows = inputs.shape[0]
    scaling = 1.0 / math.sqrt(DH)
    per_device = qkv_weight.shape[1] // lax.axis_size("col")
    local_heads = per_device // (3 * DH)
    panel_cols = qkv_weight
    packed = lax.psum_scatter(
        lax.dot_general(
            panel_cols, inputs, (((0,), (1,)), ((), ())), preferred_element_type=jnp.float32
        ),
        "col",
        scatter_dimension=0,
        tiled=True,
    ).astype(jnp.bfloat16)
    packed = packed.reshape(local_heads, 3, DH, tok_rows)
    queries = packed[:, 0]
    key_own = packed[:, 1]
    value_own = packed[:, 2]
    gathered = lax.all_gather(jnp.stack([key_own, value_own]), "ctx", axis=3, tiled=True)
    keys_all = gathered[0]
    values_all = gathered[1]
    scores = (
        jnp.einsum("hdq,hdk->hqk", queries, keys_all, preferred_element_type=jnp.float32) * scaling
    )
    row_top, row_total, softmax = softmax_rows(scores)
    softmax_low = softmax.astype(jnp.bfloat16)
    attended3 = jnp.einsum(
        "hqk,hdk->qhd", softmax_low, values_all, preferred_element_type=jnp.float32
    ).astype(jnp.bfloat16)
    attended = attended3.reshape(tok_rows, local_heads * DH)
    grad_out = out_cotangent.reshape(tok_rows, local_heads, DH)
    row_delta = jnp.sum(grad_out.astype(jnp.float32) * attended3.astype(jnp.float32), axis=2).T
    grad_soft = jnp.einsum("qhd,hdk->hqk", grad_out, values_all, preferred_element_type=jnp.float32)
    grad_score = (softmax * (grad_soft - row_delta[:, :, None])).astype(jnp.bfloat16)
    grad_query = (
        jnp.einsum("hqk,hdk->hdq", grad_score, keys_all, preferred_element_type=jnp.float32)
        * scaling
    ).astype(jnp.bfloat16)
    grad_out_t = jnp.transpose(grad_out, (1, 2, 0))
    stat_top, stat_total, stat_delta = (
        lax.all_gather(row_top, "ctx", axis=1, tiled=True),
        lax.all_gather(row_total, "ctx", axis=1, tiled=True),
        lax.all_gather(row_delta, "ctx", axis=1, tiled=True),
    )
    query_part = lax.all_gather(queries, "ctx", axis=2, tiled=True)
    grad_part = lax.all_gather(grad_out_t, "ctx", axis=2, tiled=True)
    part_scores = (
        jnp.einsum("hdq,hdk->hqk", query_part, key_own, preferred_element_type=jnp.float32)
        * scaling
    )
    part_prob = jnp.exp(part_scores - stat_top[:, :, None]) / stat_total[:, :, None]
    part_grad = jnp.einsum("hdq,hdk->hqk", grad_part, value_own, preferred_element_type=jnp.float32)
    part_score = (part_prob * (part_grad - stat_delta[:, :, None])).astype(jnp.bfloat16)
    new_key = (
        jnp.einsum("hqk,hdq->hdk", part_score, query_part, preferred_element_type=jnp.float32)
        * scaling
    )
    new_value = jnp.einsum(
        "hqk,hdq->hdk",
        part_prob.astype(jnp.bfloat16),
        grad_part,
        preferred_element_type=jnp.float32,
    )
    grad_key = new_key
    grad_value = new_value
    grad_key = grad_key.astype(jnp.bfloat16)
    grad_value = grad_value.astype(jnp.bfloat16)
    grad_packed = jnp.stack([grad_query, grad_key, grad_value], axis=1).reshape(
        local_heads * 3 * DH, tok_rows
    )
    panel_cols = qkv_weight
    local_sum = lax.dot_general(
        lax.all_gather(grad_packed, "col", axis=0, tiled=True),
        panel_cols,
        (((0,), (1,)), ((), ())),
        preferred_element_type=jnp.float32,
    )
    input_grad = lax.psum(local_sum, "row").astype(jnp.bfloat16)
    return (attended, input_grad)


MESH = pl.DeviceIdType.MESH
CHUNKS = 16
LAG = 2
NN = (((1,), (0,)), ((), ()))
NT = (((1,), (1,)), ((), ()))
TN = (((0,), (0,)), ((), ()))


def dot(a, b, dims):
    return lax.dot_general(a, b, dims, preferred_element_type=jnp.float32)


def block_kernel(
    x_ref, w_hbm, cot_ref, att_ref, grad_ref,
    w_ref, far_kv, far_q, got_kv, got_q, part_near, got_near, cot_all, query, kv, score, gscore,
    prob_low, ds_low, att_mine, att_send, att_got, dq_send, dkv_send, dkv_got, dkv_own,
    dkv_out, packed, z_own, z_edge, z_mid, z_tot, ss, rs, zs, zr, ls,
):
    tok = x_ref.shape[0]
    head = 3 * DH
    scaling = 1.0 / math.sqrt(DH)
    ctx, row, col = lax.axis_index("ctx"), lax.axis_index("row"), lax.axis_index("col")
    core = lax.rem(ctx, 2)
    far_x = lax.rem(ctx + 2, 4)
    near = ctx + 1 - 2 * core
    far_col = 1 - col
    is_mid = jnp.logical_or(row == 1, row == 2)
    mid_peer = 3 - row
    side = jnp.where(row == 0, 1, jnp.where(row == 1, 0, jnp.where(row == 2, 3, 2)))
    at_near = {"ctx": near, "row": row, "col": col}
    at_far = {"ctx": ctx, "row": row, "col": far_col}
    at_diag = {"ctx": near, "row": row, "col": far_col}
    at_x = {"ctx": far_x, "row": row, "col": col}
    at_side = {"ctx": ctx, "row": side, "col": col}
    at_mid = {"ctx": ctx, "row": mid_peer, "col": col}

    def rc(src, dst, n, dev):
        return pltpu.make_async_remote_copy(
            src_ref=src, dst_ref=dst, send_sem=ss.at[n], recv_sem=rs.at[n],
            device_id=dev, device_id_type=MESH,
        )

    def lanes(start, size):
        return pl.ds(pl.multiple_of(start, 128), size)

    far_w = lanes(far_col * 2 * head, 2 * head)
    own_w = lanes(col * 2 * head, 2 * head)
    loads = [
        pltpu.make_async_copy(w_hbm.at[:, far_w], w_ref.at[:, far_w], ls.at[0]),
        pltpu.make_async_copy(w_hbm.at[:, own_w], w_ref.at[:, own_w], ls.at[1]),
    ]
    for load in loads:
        load.start()
    barrier = pltpu.get_barrier_semaphore()
    for dev in (at_near, at_far, at_diag, at_x, at_side):
        pl.semaphore_signal(barrier, inc=1, device_id=dev, device_id_type=MESH)

    @pl.when(is_mid)
    def _():
        pl.semaphore_signal(barrier, inc=1, device_id=at_mid, device_id_type=MESH)

    loads[0].wait()
    far = dot(x_ref[...], w_ref[:, far_w], NN)
    for n in range(2):
        far_q[n] = far[:, n * head : n * head + DH]
        far_kv[n] = far[:, n * head + DH : (n + 1) * head]

    @pl.when(is_mid)
    def _():
        pl.semaphore_wait(barrier, 6)

    @pl.when(jnp.logical_not(is_mid))
    def _():
        pl.semaphore_wait(barrier, 5)

    sent = []

    def go(copy):
        copy.start()
        sent.append(copy)
        return copy

    kv_copies = [go(rc(far_kv.at[core], got_kv.at[0], 0, at_far))]
    kv_copies.append(go(rc(far_kv.at[1 - core], got_kv.at[1], 1, at_diag)))
    q_copies = [go(rc(far_q.at[core], got_q.at[0], 15, at_far))]
    q_copies.append(go(rc(far_q.at[1 - core], got_q.at[1], 16, at_diag)))
    cc = go(rc(cot_ref.at[:, lanes((1 - core) * DH, DH)], cot_all.at[pl.ds(tok, tok)], 3, at_near))
    loads[1].wait()
    own = dot(x_ref[...], w_ref[:, own_w], NN)
    part_near[0] = own[:, :head]
    part_near[1] = own[:, head:]
    near_copy = go(rc(part_near.at[1 - core], got_near, 2, at_near))
    cot_all[pl.ds(0, tok), :] = cot_ref[:, lanes(core * DH, DH)]

    kv_sent = []
    for t in range(2):
        kv_copies[t].wait_recv()
        if t == 0:
            mine = part_near[core, :, DH:]
        else:
            near_copy.wait_recv()
            mine = got_near[:, DH:]
        here = pl.ds(t * tok, tok)
        kv[here, :] = (mine + got_kv[t]).astype(jnp.bfloat16)
        kv_sent.append(go(rc(kv.at[here], kv.at[pl.ds((2 + t) * tok, tok)], 4 + t, at_x)))

    cc.wait_recv()
    near_keys = pl.ds(0, 2 * tok)
    far_keys = pl.ds(2 * tok, 2 * tok)
    gscore[:, near_keys] = dot(cot_all[...], kv[near_keys, DH:], NT)
    for t in range(2):
        q_copies[t].wait_recv()
        mine = part_near[core, :, :DH] if t == 0 else got_near[:, :DH]
        query[pl.ds(t * tok, tok), :] = (mine + got_q[t]).astype(jnp.bfloat16)
    score[:, near_keys] = dot(query[...], kv[near_keys, :DH], NT) * scaling
    for t in range(2):
        kv_sent[t].wait_recv()
    gscore[:, far_keys] = dot(cot_all[...], kv[far_keys, DH:], NT)
    score[:, far_keys] = dot(query[...], kv[far_keys, :DH], NT) * scaling

    mine_lane = (2 * col + core) * head
    part = tok // 2
    for t in (1, 0):
        for half in range(2):
            here = pl.ds(t * tok + half * part, part)
            local = pl.ds(half * part, part)
            s = score[here, :]
            e = jnp.exp(s - jnp.max(s, axis=1, keepdims=True))
            p = e * (1.0 / jnp.sum(e, axis=1, keepdims=True))
            low = p.astype(jnp.bfloat16)
            prob_low[here, :] = low
            att = dot(low, kv[:, DH:], NN).astype(jnp.bfloat16)
            delta = jnp.sum(
                cot_all[here, :].astype(jnp.float32) * att.astype(jnp.float32), axis=1, keepdims=True
            )
            ds = (p * (gscore[here, :] - delta)).astype(jnp.bfloat16)
            ds_low[here, :] = ds
            if t == 1:
                att_send[local, :] = att
            else:
                att_mine[local, :] = att

    dkv_copies = []
    for t in range(2):
        keys = pl.ds((2 + t) * tok, tok)
        here = pl.ds(t * tok, tok)
        dkv_send[here, :DH] = (dot(ds_low[:, keys], query[...], TN) * scaling).astype(jnp.bfloat16)
        dkv_send[here, DH:] = dot(prob_low[:, keys], cot_all[...], TN).astype(jnp.bfloat16)
        dkv_copies.append(go(rc(dkv_send.at[here], dkv_got.at[here], 6 + t, at_x)))
    for t in (1, 0):
        here = pl.ds(t * tok, tok)
        slot = packed.at[:, lanes(mine_lane, DH)]
        dq_send[here, :] = (dot(ds_low[here, :], kv[:, :DH], NN) * scaling).astype(jnp.bfloat16)
        if t == 1:
            go(rc(dq_send.at[here], slot, 9, at_diag))
            go(rc(dq_send.at[here], slot, 10, at_near))
            att_copy = go(rc(att_send, att_got, 8, at_near))
        else:
            go(rc(dq_send.at[here], slot, 11, at_far))
            packed[:, lanes(mine_lane, DH)] = dq_send[here, :]
    dkv_own[:, :DH] = dot(ds_low[:, near_keys], query[...], TN) * scaling
    dkv_own[:, DH:] = dot(prob_low[:, near_keys], cot_all[...], TN)
    att_copy.wait_recv()
    att_ref[:, lanes(core * DH, DH)] = att_mine[...]
    att_ref[:, lanes((1 - core) * DH, DH)] = att_got[...]
    slot = packed.at[:, lanes(mine_lane + DH, 2 * DH)]
    for t in (0, 1):
        here = pl.ds(t * tok, tok)
        dkv_copies[t].wait_recv()
        dkv_out[here, :] = (dkv_own[here, :] + dkv_got[here, :].astype(jnp.float32)).astype(jnp.bfloat16)
        if t == 1:
            go(rc(dkv_out.at[here], slot, 12, at_diag))
            go(rc(dkv_out.at[here], slot, 13, at_near))
        else:
            go(rc(dkv_out.at[here], slot, 14, at_far))
            packed[:, lanes(mine_lane + DH, 2 * DH)] = dkv_out[here, :]

    near_lane = (2 * col + 1 - core) * head
    far_lane = (2 * far_col + core) * head
    diag_lane = (2 * far_col + 1 - core) * head
    for n_q, n_kv, lane, dev in (
        (10, 13, near_lane, at_near), (11, 14, far_lane, at_far), (9, 12, diag_lane, at_diag)
    ):
        to = packed.at[:, lanes(lane, DH)]
        rc(to, to, n_q, dev).wait_recv()
        to = packed.at[:, lanes(lane + DH, 2 * DH)]
        rc(to, to, n_kv, dev).wait_recv()

    width = grad_ref.shape[1] // CHUNKS

    def zcopy(kind, src, dst, k, dev):
        return pltpu.make_async_remote_copy(
            src_ref=src.at[k], dst_ref=dst.at[k], send_sem=zs.at[kind, k], recv_sem=zr.at[kind, k],
            device_id=dev, device_id_type=MESH,
        )

    def product(k):
        rows = pl.ds(pl.multiple_of(k * width, width), width)
        return dot(packed[...], w_ref[rows, :], NT)

    def put(k, value):
        grad_ref[:, lanes(k * width, width)] = value

    @pl.when(jnp.logical_not(is_mid))
    def _():
        @pl.loop(0, CHUNKS)
        def _(k):
            z_own[k] = product(k).astype(jnp.bfloat16)
            zcopy(0, z_own, z_edge, k, at_side).start()

        @pl.loop(0, CHUNKS)
        def _(k):
            zcopy(2, z_tot, z_tot, k, at_side).wait_recv()
            put(k, z_tot[k])
            zcopy(0, z_own, z_edge, k, at_side).wait_send()

    @pl.when(is_mid)
    def _():
        def finish(k):
            zcopy(1, z_own, z_mid, k, at_mid).wait_recv()
            total = (z_own[k].astype(jnp.float32) + z_mid[k].astype(jnp.float32)).astype(jnp.bfloat16)
            z_tot[k] = total
            zcopy(2, z_tot, z_tot, k, at_side).start()
            put(k, total)

        @pl.loop(0, CHUNKS)
        def _(k):
            term = product(k)
            zcopy(0, z_own, z_edge, k, at_side).wait_recv()
            z_own[k] = (term + z_edge[k].astype(jnp.float32)).astype(jnp.bfloat16)
            zcopy(1, z_own, z_mid, k, at_mid).start()

            @pl.when(k >= LAG)
            def _():
                finish(k - LAG)

        @pl.loop(CHUNKS - LAG, CHUNKS)
        def _(k):
            finish(k)

        @pl.loop(0, CHUNKS)
        def _(k):
            zcopy(1, z_own, z_mid, k, at_mid).wait_send()
            zcopy(2, z_tot, z_tot, k, at_side).wait_send()

    for copy in sent:
        copy.wait_send()


def fused(inputs, qkv_weight, out_cotangent):
    tok, wide = inputs.shape
    low, full = jnp.bfloat16, jnp.float32
    head = 3 * DH
    chunk = (CHUNKS, tok, wide // CHUNKS)
    vmem = pl.BlockSpec(memory_space=pltpu.VMEM)
    shapes = [
        (qkv_weight.shape, low),
        ((2, tok, 2 * DH), full), ((2, tok, DH), full), ((2, tok, 2 * DH), full), ((2, tok, DH), full),
        ((2, tok, head), full), ((tok, head), full),
        ((2 * tok, DH), low), ((2 * tok, DH), low), ((4 * tok, 2 * DH), low),
        ((2 * tok, 4 * tok), full), ((2 * tok, 4 * tok), full),
        ((2 * tok, 4 * tok), low), ((2 * tok, 4 * tok), low),
        ((tok, DH), low), ((tok, DH), low), ((tok, DH), low), ((2 * tok, DH), low),
        ((2 * tok, 2 * DH), low), ((2 * tok, 2 * DH), low), ((2 * tok, 2 * DH), full),
        ((2 * tok, 2 * DH), low), ((tok, 4 * head), low),
        (chunk, low), (chunk, low), (chunk, low), (chunk, low),
    ]
    return pl.pallas_call(
        block_kernel,
        out_shape=(
            jax.ShapeDtypeStruct(out_cotangent.shape, low),
            jax.ShapeDtypeStruct(inputs.shape, low),
        ),
        in_specs=[vmem, pl.BlockSpec(memory_space=pl.ANY), vmem],
        out_specs=(vmem, vmem),
        scratch_shapes=[pltpu.VMEM(shape, kind) for shape, kind in shapes]
        + [pltpu.SemaphoreType.DMA((17,))] * 2
        + [pltpu.SemaphoreType.DMA((3, CHUNKS))] * 2
        + [pltpu.SemaphoreType.DMA((2,))],
        compiler_params=pltpu.CompilerParams(
            collective_id=0, has_side_effects=True, vmem_limit_bytes=48 * 1024 * 1024
        ),
    )(inputs, qkv_weight, out_cotangent)


def block(inputs, qkv_weight, out_cotangent):
    sizes = tuple(lax.axis_size(name) for name in ("ctx", "row", "col"))
    heads = qkv_weight.shape[1] // (3 * DH)
    if sizes == (4, 4, 2) and heads == 4 and inputs.shape[0] <= 256:
        return fused(inputs, qkv_weight, out_cotangent)
    return shards(inputs, qkv_weight, out_cotangent)


def solution(mesh):
    return jax.shard_map(
        block,
        mesh=mesh,
        in_specs=(P("ctx", "col"), P("col", "row"), P("ctx", ("row", "col"))),
        out_specs=(P("ctx", ("row", "col")), P("ctx", "col")),
        check_vma=False,
    )
```

```python
import math

import jax
import jax.numpy as jnp
from jax import lax
from jax.experimental import pallas as pl
from jax.experimental.pallas import tpu as pltpu
from jax.sharding import PartitionSpec as P

DH = 128


def softmax_rows(scores):
    row_top = jnp.max(scores, axis=2)
    expo_vals = jnp.exp(scores - row_top[:, :, None])
    row_total = jnp.sum(expo_vals, axis=2)
    return (row_top, row_total, expo_vals / row_total[:, :, None])


def shards(inputs, qkv_weight, out_cotangent):
    tok_rows = inputs.shape[0]
    scaling = 1.0 / math.sqrt(DH)
    per_device = qkv_weight.shape[1] // lax.axis_size("col")
    local_heads = per_device // (3 * DH)
    panel_cols = qkv_weight
    packed = lax.psum_scatter(
        lax.dot_general(
            panel_cols, inputs, (((0,), (1,)), ((), ())), preferred_element_type=jnp.float32
        ),
        "col",
        scatter_dimension=0,
        tiled=True,
    ).astype(jnp.bfloat16)
    packed = packed.reshape(local_heads, 3, DH, tok_rows)
    queries = packed[:, 0]
    key_own = packed[:, 1]
    value_own = packed[:, 2]
    gathered = lax.all_gather(jnp.stack([key_own, value_own]), "ctx", axis=3, tiled=True)
    keys_all = gathered[0]
    values_all = gathered[1]
    scores = (
        jnp.einsum("hdq,hdk->hqk", queries, keys_all, preferred_element_type=jnp.float32) * scaling
    )
    row_top, row_total, softmax = softmax_rows(scores)
    softmax_low = softmax.astype(jnp.bfloat16)
    attended3 = jnp.einsum(
        "hqk,hdk->qhd", softmax_low, values_all, preferred_element_type=jnp.float32
    ).astype(jnp.bfloat16)
    attended = attended3.reshape(tok_rows, local_heads * DH)
    grad_out = out_cotangent.reshape(tok_rows, local_heads, DH)
    row_delta = jnp.sum(grad_out.astype(jnp.float32) * attended3.astype(jnp.float32), axis=2).T
    grad_soft = jnp.einsum("qhd,hdk->hqk", grad_out, values_all, preferred_element_type=jnp.float32)
    grad_score = (softmax * (grad_soft - row_delta[:, :, None])).astype(jnp.bfloat16)
    grad_query = (
        jnp.einsum("hqk,hdk->hdq", grad_score, keys_all, preferred_element_type=jnp.float32)
        * scaling
    ).astype(jnp.bfloat16)
    grad_out_t = jnp.transpose(grad_out, (1, 2, 0))
    stat_top, stat_total, stat_delta = (
        lax.all_gather(row_top, "ctx", axis=1, tiled=True),
        lax.all_gather(row_total, "ctx", axis=1, tiled=True),
        lax.all_gather(row_delta, "ctx", axis=1, tiled=True),
    )
    query_part = lax.all_gather(queries, "ctx", axis=2, tiled=True)
    grad_part = lax.all_gather(grad_out_t, "ctx", axis=2, tiled=True)
    part_scores = (
        jnp.einsum("hdq,hdk->hqk", query_part, key_own, preferred_element_type=jnp.float32)
        * scaling
    )
    part_prob = jnp.exp(part_scores - stat_top[:, :, None]) / stat_total[:, :, None]
    part_grad = jnp.einsum("hdq,hdk->hqk", grad_part, value_own, preferred_element_type=jnp.float32)
    part_score = (part_prob * (part_grad - stat_delta[:, :, None])).astype(jnp.bfloat16)
    new_key = (
        jnp.einsum("hqk,hdq->hdk", part_score, query_part, preferred_element_type=jnp.float32)
        * scaling
    )
    new_value = jnp.einsum(
        "hqk,hdq->hdk",
        part_prob.astype(jnp.bfloat16),
        grad_part,
        preferred_element_type=jnp.float32,
    )
    grad_key = new_key
    grad_value = new_value
    grad_key = grad_key.astype(jnp.bfloat16)
    grad_value = grad_value.astype(jnp.bfloat16)
    grad_packed = jnp.stack([grad_query, grad_key, grad_value], axis=1).reshape(
        local_heads * 3 * DH, tok_rows
    )
    panel_cols = qkv_weight
    local_sum = lax.dot_general(
        lax.all_gather(grad_packed, "col", axis=0, tiled=True),
        panel_cols,
        (((0,), (1,)), ((), ())),
        preferred_element_type=jnp.float32,
    )
    input_grad = lax.psum(local_sum, "row").astype(jnp.bfloat16)
    return (attended, input_grad)


MESH = pl.DeviceIdType.MESH
CHUNKS = 16
LAG = 2
NN = (((1,), (0,)), ((), ()))
NT = (((1,), (1,)), ((), ()))
TN = (((0,), (0,)), ((), ()))


def dot(a, b, dims):
    return lax.dot_general(a, b, dims, preferred_element_type=jnp.float32)


def block_kernel(
    x_ref, w_hbm, cot_ref, att_ref, grad_ref,
    w_ref, far_kv, far_q, got_kv, got_q, part_near, got_near, cot_all, query, kv, score, gscore,
    prob_low, ds_low, att_mine, att_send, att_got, dq_send, dkv_send, dkv_got, dkv_own,
    dkv_out, packed, z_own, z_edge, z_mid, z_tot, ss, rs, zs, zr, ls,
):
    tok = x_ref.shape[0]
    head = 3 * DH
    scaling = 1.0 / math.sqrt(DH)
    ctx, row, col = lax.axis_index("ctx"), lax.axis_index("row"), lax.axis_index("col")
    core = lax.rem(ctx, 2)
    far_x = lax.rem(ctx + 2, 4)
    near = ctx + 1 - 2 * core
    far_col = 1 - col
    is_mid = jnp.logical_or(row == 1, row == 2)
    mid_peer = 3 - row
    side = jnp.where(row == 0, 1, jnp.where(row == 1, 0, jnp.where(row == 2, 3, 2)))
    at_near = {"ctx": near, "row": row, "col": col}
    at_far = {"ctx": ctx, "row": row, "col": far_col}
    at_diag = {"ctx": near, "row": row, "col": far_col}
    at_x = {"ctx": far_x, "row": row, "col": col}
    at_side = {"ctx": ctx, "row": side, "col": col}
    at_mid = {"ctx": ctx, "row": mid_peer, "col": col}

    def rc(src, dst, n, dev):
        return pltpu.make_async_remote_copy(
            src_ref=src, dst_ref=dst, send_sem=ss.at[n], recv_sem=rs.at[n],
            device_id=dev, device_id_type=MESH,
        )

    def lanes(start, size):
        return pl.ds(pl.multiple_of(start, 128), size)

    far_heads = ((2 * far_col + core) * head, (2 * far_col + 1 - core) * head)
    far_parts = [lanes(n + DH, 2 * DH) for n in far_heads] + [lanes(n, DH) for n in far_heads]
    own_w = lanes(col * 2 * head, 2 * head)
    loads = [
        pltpu.make_async_copy(w_hbm.at[:, part], w_ref.at[:, part], ls.at[n])
        for n, part in enumerate(far_parts + [own_w])
    ]
    for load in loads:
        load.start()
    barrier = pltpu.get_barrier_semaphore()
    for dev in (at_near, at_far, at_diag, at_x, at_side):
        pl.semaphore_signal(barrier, inc=1, device_id=dev, device_id_type=MESH)

    @pl.when(is_mid)
    def _():
        pl.semaphore_signal(barrier, inc=1, device_id=at_mid, device_id_type=MESH)

    loads[0].wait()
    far_kv[0] = dot(x_ref[...], w_ref[:, far_parts[0]], NN)

    @pl.when(is_mid)
    def _():
        pl.semaphore_wait(barrier, 6)

    @pl.when(jnp.logical_not(is_mid))
    def _():
        pl.semaphore_wait(barrier, 5)

    sent = []

    def go(copy):
        copy.start()
        sent.append(copy)
        return copy

    kv_copies = [go(rc(far_kv.at[0], got_kv.at[0], 0, at_far))]
    loads[1].wait()
    far_kv[1] = dot(x_ref[...], w_ref[:, far_parts[1]], NN)
    kv_copies.append(go(rc(far_kv.at[1], got_kv.at[1], 1, at_diag)))
    q_copies = []
    for n, dev in enumerate((at_far, at_diag)):
        loads[2 + n].wait()
        far_q[n] = dot(x_ref[...], w_ref[:, far_parts[2 + n]], NN)
        q_copies.append(go(rc(far_q.at[n], got_q.at[n], 15 + n, dev)))
    cc = go(rc(cot_ref.at[:, lanes((1 - core) * DH, DH)], cot_all.at[pl.ds(tok, tok)], 3, at_near))
    loads[4].wait()
    own = dot(x_ref[...], w_ref[:, own_w], NN)
    part_near[0] = own[:, :head]
    part_near[1] = own[:, head:]
    near_copy = go(rc(part_near.at[1 - core], got_near, 2, at_near))
    cot_all[pl.ds(0, tok), :] = cot_ref[:, lanes(core * DH, DH)]

    kv_sent = []
    for t in range(2):
        kv_copies[t].wait_recv()
        if t == 0:
            mine = part_near[core, :, DH:]
        else:
            near_copy.wait_recv()
            mine = got_near[:, DH:]
        here = pl.ds(t * tok, tok)
        kv[here, :] = (mine + got_kv[t]).astype(jnp.bfloat16)
        kv_sent.append(go(rc(kv.at[here], kv.at[pl.ds((2 + t) * tok, tok)], 4 + t, at_x)))

    cc.wait_recv()
    near_keys = pl.ds(0, 2 * tok)
    far_keys = pl.ds(2 * tok, 2 * tok)
    gscore[:, near_keys] = dot(cot_all[...], kv[near_keys, DH:], NT)
    for t in range(2):
        q_copies[t].wait_recv()
        mine = part_near[core, :, :DH] if t == 0 else got_near[:, :DH]
        query[pl.ds(t * tok, tok), :] = (mine + got_q[t]).astype(jnp.bfloat16)
    score[:, near_keys] = dot(query[...], kv[near_keys, :DH], NT) * scaling
    for t in range(2):
        kv_sent[t].wait_recv()
    gscore[:, far_keys] = dot(cot_all[...], kv[far_keys, DH:], NT)
    score[:, far_keys] = dot(query[...], kv[far_keys, :DH], NT) * scaling

    mine_lane = (2 * col + core) * head
    part = tok // 2
    for t in (1, 0):
        for half in range(2):
            here = pl.ds(t * tok + half * part, part)
            local = pl.ds(half * part, part)
            s = score[here, :]
            e = jnp.exp(s - jnp.max(s, axis=1, keepdims=True))
            p = e * (1.0 / jnp.sum(e, axis=1, keepdims=True))
            low = p.astype(jnp.bfloat16)
            prob_low[here, :] = low
            att = dot(low, kv[:, DH:], NN).astype(jnp.bfloat16)
            delta = jnp.sum(
                cot_all[here, :].astype(jnp.float32) * att.astype(jnp.float32), axis=1, keepdims=True
            )
            ds = (p * (gscore[here, :] - delta)).astype(jnp.bfloat16)
            ds_low[here, :] = ds
            if t == 1:
                att_send[local, :] = att
            else:
                att_mine[local, :] = att

    dkv_copies = []
    for t in range(2):
        keys = pl.ds((2 + t) * tok, tok)
        here = pl.ds(t * tok, tok)
        dkv_send[here, :DH] = (dot(ds_low[:, keys], query[...], TN) * scaling).astype(jnp.bfloat16)
        dkv_send[here, DH:] = dot(prob_low[:, keys], cot_all[...], TN).astype(jnp.bfloat16)
        dkv_copies.append(go(rc(dkv_send.at[here], dkv_got.at[here], 6 + t, at_x)))
    for t in (1, 0):
        here = pl.ds(t * tok, tok)
        slot = packed.at[:, lanes(mine_lane, DH)]
        dq_send[here, :] = (dot(ds_low[here, :], kv[:, :DH], NN) * scaling).astype(jnp.bfloat16)
        if t == 1:
            go(rc(dq_send.at[here], slot, 9, at_diag))
            go(rc(dq_send.at[here], slot, 10, at_near))
            att_copy = go(rc(att_send, att_got, 8, at_near))
        else:
            go(rc(dq_send.at[here], slot, 11, at_far))
            packed[:, lanes(mine_lane, DH)] = dq_send[here, :]
    dkv_own[:, :DH] = dot(ds_low[:, near_keys], query[...], TN) * scaling
    dkv_own[:, DH:] = dot(prob_low[:, near_keys], cot_all[...], TN)
    att_copy.wait_recv()
    att_ref[:, lanes(core * DH, DH)] = att_mine[...]
    att_ref[:, lanes((1 - core) * DH, DH)] = att_got[...]
    slot = packed.at[:, lanes(mine_lane + DH, 2 * DH)]
    for t in (0, 1):
        here = pl.ds(t * tok, tok)
        dkv_copies[t].wait_recv()
        dkv_out[here, :] = (dkv_own[here, :] + dkv_got[here, :].astype(jnp.float32)).astype(jnp.bfloat16)
        if t == 1:
            go(rc(dkv_out.at[here], slot, 12, at_diag))
            go(rc(dkv_out.at[here], slot, 13, at_near))
        else:
            go(rc(dkv_out.at[here], slot, 14, at_far))
            packed[:, lanes(mine_lane + DH, 2 * DH)] = dkv_out[here, :]

    near_lane = (2 * col + 1 - core) * head
    far_lane = (2 * far_col + core) * head
    diag_lane = (2 * far_col + 1 - core) * head
    for n_q, n_kv, lane, dev in (
        (10, 13, near_lane, at_near), (11, 14, far_lane, at_far), (9, 12, diag_lane, at_diag)
    ):
        to = packed.at[:, lanes(lane, DH)]
        rc(to, to, n_q, dev).wait_recv()
        to = packed.at[:, lanes(lane + DH, 2 * DH)]
        rc(to, to, n_kv, dev).wait_recv()

    width = grad_ref.shape[1] // CHUNKS

    def zcopy(kind, src, dst, k, dev):
        return pltpu.make_async_remote_copy(
            src_ref=src.at[k], dst_ref=dst.at[k], send_sem=zs.at[kind, k], recv_sem=zr.at[kind, k],
            device_id=dev, device_id_type=MESH,
        )

    def product(k):
        rows = pl.ds(pl.multiple_of(k * width, width), width)
        return dot(packed[...], w_ref[rows, :], NT)

    def put(k, value):
        grad_ref[:, lanes(k * width, width)] = value

    @pl.when(jnp.logical_not(is_mid))
    def _():
        @pl.loop(0, CHUNKS)
        def _(k):
            z_own[k] = product(k).astype(jnp.bfloat16)
            zcopy(0, z_own, z_edge, k, at_side).start()

        @pl.loop(0, CHUNKS)
        def _(k):
            zcopy(2, z_tot, z_tot, k, at_side).wait_recv()
            put(k, z_tot[k])
            zcopy(0, z_own, z_edge, k, at_side).wait_send()

    @pl.when(is_mid)
    def _():
        def finish(k):
            zcopy(1, z_own, z_mid, k, at_mid).wait_recv()
            total = (z_own[k].astype(jnp.float32) + z_mid[k].astype(jnp.float32)).astype(jnp.bfloat16)
            z_tot[k] = total
            zcopy(2, z_tot, z_tot, k, at_side).start()
            put(k, total)

        @pl.loop(0, CHUNKS)
        def _(k):
            term = product(k)
            zcopy(0, z_own, z_edge, k, at_side).wait_recv()
            z_own[k] = (term + z_edge[k].astype(jnp.float32)).astype(jnp.bfloat16)
            zcopy(1, z_own, z_mid, k, at_mid).start()

            @pl.when(k >= LAG)
            def _():
                finish(k - LAG)

        @pl.loop(CHUNKS - LAG, CHUNKS)
        def _(k):
            finish(k)

        @pl.loop(0, CHUNKS)
        def _(k):
            zcopy(1, z_own, z_mid, k, at_mid).wait_send()
            zcopy(2, z_tot, z_tot, k, at_side).wait_send()

    for copy in sent:
        copy.wait_send()


def fused(inputs, qkv_weight, out_cotangent):
    tok, wide = inputs.shape
    low, full = jnp.bfloat16, jnp.float32
    head = 3 * DH
    chunk = (CHUNKS, tok, wide // CHUNKS)
    vmem = pl.BlockSpec(memory_space=pltpu.VMEM)
    shapes = [
        (qkv_weight.shape, low),
        ((2, tok, 2 * DH), full), ((2, tok, DH), full), ((2, tok, 2 * DH), full), ((2, tok, DH), full),
        ((2, tok, head), full), ((tok, head), full),
        ((2 * tok, DH), low), ((2 * tok, DH), low), ((4 * tok, 2 * DH), low),
        ((2 * tok, 4 * tok), full), ((2 * tok, 4 * tok), full),
        ((2 * tok, 4 * tok), low), ((2 * tok, 4 * tok), low),
        ((tok, DH), low), ((tok, DH), low), ((tok, DH), low), ((2 * tok, DH), low),
        ((2 * tok, 2 * DH), low), ((2 * tok, 2 * DH), low), ((2 * tok, 2 * DH), full),
        ((2 * tok, 2 * DH), low), ((tok, 4 * head), low),
        (chunk, low), (chunk, low), (chunk, low), (chunk, low),
    ]
    return pl.pallas_call(
        block_kernel,
        out_shape=(
            jax.ShapeDtypeStruct(out_cotangent.shape, low),
            jax.ShapeDtypeStruct(inputs.shape, low),
        ),
        in_specs=[vmem, pl.BlockSpec(memory_space=pl.ANY), vmem],
        out_specs=(vmem, vmem),
        scratch_shapes=[pltpu.VMEM(shape, kind) for shape, kind in shapes]
        + [pltpu.SemaphoreType.DMA((17,))] * 2
        + [pltpu.SemaphoreType.DMA((3, CHUNKS))] * 2
        + [pltpu.SemaphoreType.DMA((5,))],
        compiler_params=pltpu.CompilerParams(
            collective_id=0, has_side_effects=True, vmem_limit_bytes=48 * 1024 * 1024
        ),
    )(inputs, qkv_weight, out_cotangent)


def block(inputs, qkv_weight, out_cotangent):
    sizes = tuple(lax.axis_size(name) for name in ("ctx", "row", "col"))
    heads = qkv_weight.shape[1] // (3 * DH)
    if sizes == (4, 4, 2) and heads == 4 and inputs.shape[0] <= 256:
        return fused(inputs, qkv_weight, out_cotangent)
    return shards(inputs, qkv_weight, out_cotangent)


def solution(mesh):
    return jax.shard_map(
        block,
        mesh=mesh,
        in_specs=(P("ctx", "col"), P("col", "row"), P("ctx", ("row", "col"))),
        out_specs=(P("ctx", ("row", "col")), P("ctx", "col")),
        check_vma=False,
    )
```
